32 devices in a mesh: blk: 8 (over y, x, core), sub: 4 (over z).
Axes of the slice: x: 2, y: 2, z: 4, core: 2. Of those that a mesh axis runs over, the one named last changes fastest.
Arguments:
- features: float32 [1024, 512], P(('blk', 'sub')), may hold values from -3 to 3
- lengthscale: float32 [512], replicated, may hold values from 0.7 to 1.4
- probes: float32 [1024, 64], P(('blk', 'sub')), may hold values from -6 to 6
- cotangent: float32 [1024, 64], P(('blk', 'sub')), may hold values from -1.5 to 1.5
Outputs:
- product: float32 [1024, 64], P(('blk', 'sub'))
- scaled_grad: float32 [1024, 512], P(('blk', 'sub'))
The draws below stay inside these ranges and needn't reach their ends.
All inputs are finite; a program needn't handle non-finite values.
Results may differ from the reference program's by a relative error of at most 0.0003.
Values sent between devices are 32-bit elements; how exact they have to be, the bound alone decides.
No kernel may reach another device: no remote copies, remote signals or barrier semaphores. Data moves between devices by JAX's collectives and lax.ppermute only.
A program may use at most 64 MiB of HBM per device.

```python
import math
import jax
import jax.numpy as jnp
from jax import lax

F = 512
P_SIZE = 64
NB = 128
NPTS = 1024
N_BLK = 8


latent_count = 8


def draw_features(key, part):
    key_latent = jax.random.fold_in(key, 101)
    key_mixing = jax.random.fold_in(key, 202)
    key_noise = jax.random.fold_in(key, 303)
    latent = jnp.clip(jax.random.normal(key_latent, (NPTS, latent_count), jnp.float32), -4.0, 4.0)
    row_scale = jnp.ones((NPTS, 1), jnp.float32)
    mixing = jnp.clip(jax.random.normal(key_mixing, (latent_count, F), jnp.float32), -4.0, 4.0) / math.sqrt(F)
    noise = jnp.clip(jax.random.normal(key_noise, (NPTS, F), jnp.float32), -4.0, 4.0) * (row_scale / math.sqrt(F))
    mapped = jnp.dot(latent, mixing, precision=lax.Precision.HIGHEST, preferred_element_type=jnp.float32)
    return jnp.clip(mapped + noise, -3.0, 3.0).astype(jnp.float32)


def shard_levels(stream_key, extent, shards, low, largest):
    factor_of = 1.0
    for dim, parts in shards:
        draws = jax.random.uniform(jax.random.fold_in(jax.random.fold_in(stream_key, 6), dim), (parts,), jnp.float32, low / len(shards), largest / len(shards))
        factor_of = factor_of * jnp.repeat(jnp.exp(draws), extent[dim] // parts).reshape((-1,) + (1,) * (len(extent) - 1 - dim))
    return factor_of


def bell_draw(key, extent, width, most, pieces=(), kind=jnp.bfloat16):
    drawn = jax.random.normal(key, extent, jnp.float32) * width
    if len(pieces) > 0:
        drawn = shard_levels(key, extent, pieces, -0.22, 0.18) * drawn
    return jnp.clip(drawn, min=-most, max=most).astype(kind)


def setup_inputs(seed: int = 0) -> dict:
    splits = jax.random.split(jax.random.key(seed), 5)
    return {
        "features": draw_features(jax.random.fold_in(splits[4], 71), 0),
        "lengthscale": jnp.clip(jnp.exp(jax.random.uniform(splits[1], (F,), jnp.float32, math.log(0.7), math.log(1.4))), 0.7, 1.4),
        "probes": bell_draw(splits[2], (NPTS, P_SIZE), 1.0, 6.0, ((0, 32),), jnp.float32),
        "cotangent": bell_draw(splits[3], (NPTS, P_SIZE), 0.25, 1.5, ((0, 32),), jnp.float32),
    }


HIGH = lax.Precision.HIGHEST


def reference(features, lengthscale, probes, cotangent):
    scaled = features / lengthscale[None, :]
    norms = jnp.sum(scaled * scaled, axis=1)
    pairs = jnp.concatenate([probes, cotangent], axis=1)
    swapped = jnp.concatenate([cotangent, probes], axis=1)

    def one_block(inputs):
        block_scaled, block_norms, block_pairs = inputs
        inner = jnp.dot(block_scaled, scaled.T, precision=HIGH, preferred_element_type=jnp.float32)
        kernel = jnp.exp(-0.5 * (block_norms[:, None] + norms[None, :] - 2.0 * inner))
        cross = jnp.dot(block_pairs, swapped.T, precision=HIGH, preferred_element_type=jnp.float32)
        weight = kernel * cross
        block_product = jnp.dot(kernel, probes, precision=HIGH, preferred_element_type=jnp.float32)
        block_gradient = jnp.dot(weight, scaled, precision=HIGH, preferred_element_type=jnp.float32)
        block_gradient = block_gradient - jnp.sum(weight, axis=1)[:, None] * block_scaled
        return block_product, block_gradient

    product, gradient = lax.map(one_block, (scaled.reshape(N_BLK, NB, F), norms.reshape(N_BLK, NB), pairs.reshape(N_BLK, NB, 2 * P_SIZE)))
    return product.reshape(NPTS, P_SIZE), gradient.reshape(NPTS, F)
```

```python
import jax
import jax.numpy as jnp
from jax import lax
from jax.sharding import PartitionSpec as P

HIGH = lax.Precision.HIGHEST
ROWS_RULE = (((1,), (1,)), ((), ()))
CORES = 2


def partner(position, step, length):
    if length & (length - 1) == 0:
        return position ^ step
    return (position + step) % length


def over_plane(value, step, back=False):
    blocks = lax.axis_size("blk")
    places = blocks // CORES
    pairs = [
        (p * CORES + c, partner(p, step, places) * CORES + c)
        for p in range(places)
        for c in range(CORES)
    ]
    return lax.ppermute(value, "blk", [(b, a) for a, b in pairs] if back else pairs)


def over_line(value, step):
    length = lax.axis_size("sub")
    return lax.ppermute(value, "sub", [(p, partner(p, step, length)) for p in range(length)])


def over_cores(value):
    return lax.ppermute(value, "blk", [(i, i ^ 1) for i in range(lax.axis_size("blk"))])


def on_device(features, lengthscale, probes, cotangent):
    width, probe_count = features.shape[1], probes.shape[1]
    points = features.shape[0]
    places, length = lax.axis_size("blk") // CORES, lax.axis_size("sub")
    scaled = features / lengthscale[None, :]
    data = jnp.concatenate([scaled, probes, cotangent], axis=1)
    line = [data] + [over_line(data, step) for step in range(length - 1, 0, -1)]
    plane = [data] + [over_plane(data, step) for step in range(places - 1, 0, -1)]
    near = jnp.concatenate(line, axis=0)
    columns = jnp.concatenate([near, over_cores(near)], axis=0)
    rows = jnp.concatenate(plane, axis=0)
    row_scaled, column_scaled = rows[:, :width], columns[:, :width]
    row_norms = jnp.sum(row_scaled * row_scaled, axis=1)
    column_norms = jnp.sum(column_scaled * column_scaled, axis=1)
    inner = lax.dot_general(
        row_scaled, column_scaled, ROWS_RULE, precision=HIGH, preferred_element_type=jnp.float32
    )
    kernel = jnp.exp(-0.5 * (row_norms[:, None] + column_norms[None, :] - 2.0 * inner))
    column_probes = columns[:, width : width + probe_count]
    swapped = jnp.concatenate([columns[:, width + probe_count :], column_probes], axis=1)
    cross = lax.dot_general(
        rows[:, width:], swapped, ROWS_RULE, precision=HIGH, preferred_element_type=jnp.float32
    )
    weight = kernel * cross
    product = jnp.dot(kernel, column_probes, precision=HIGH, preferred_element_type=jnp.float32)
    gradient = jnp.dot(weight, column_scaled, precision=HIGH, preferred_element_type=jnp.float32)
    gradient = gradient - jnp.sum(weight, axis=1)[:, None] * row_scaled
    partial = jnp.concatenate([gradient, product], axis=1)
    total = partial[:points]
    for place, step in enumerate(range(places - 1, 0, -1), 1):
        total = total + over_plane(partial[place * points : (place + 1) * points], step, True)
    return (total[:, width:], total[:, :width])


def solution(mesh):
    spec = P(("blk", "sub"), None)
    return jax.shard_map(
        on_device, mesh=mesh, in_specs=(spec, P(), spec, spec), out_specs=(spec, spec), check_vma=False
    )
```

```python
import functools

import jax
import jax.numpy as jnp
from jax import lax
from jax.experimental import pallas as pl
from jax.experimental.pallas import tpu as pltpu
from jax.sharding import PartitionSpec as P

HIGH = lax.Precision.HIGHEST
ROWS_RULE = (((1,), (1,)), ((), ()))
PLAIN_RULE = (((1,), (0,)), ((), ()))
CORES = 2
MIB = 2**20


def whole(count):
    return [pl.BlockSpec(memory_space=pltpu.VMEM)] * count


def dot(left, right, rule=PLAIN_RULE):
    return lax.dot_general(left, right, rule, precision=HIGH, preferred_element_type=jnp.float32)


def partner(position, step, length):
    if length & (length - 1) == 0:
        return position ^ step
    return (position + step) % length


def over_plane(value, step, back=False):
    blocks = lax.axis_size("blk")
    places = blocks // CORES
    pairs = [
        (p * CORES + c, partner(p, step, places) * CORES + c)
        for p in range(places)
        for c in range(CORES)
    ]
    return lax.ppermute(value, "blk", [(b, a) for a, b in pairs] if back else pairs)


def over_line(value, step):
    length = lax.axis_size("sub")
    return lax.ppermute(value, "sub", [(p, partner(p, step, length)) for p in range(length)])


def over_cores(value):
    return lax.ppermute(value, "blk", [(i, i ^ 1) for i in range(lax.axis_size("blk"))])


def gathered_line(value):
    length = lax.axis_size("sub")
    if length & (length - 1):
        return [value] + [over_line(value, step) for step in range(length - 1, 0, -1)]
    pieces, step = [value], length // 2
    while step:
        pieces = pieces + [over_line(piece, step) for piece in pieces]
        step //= 2
    return pieces


def stage_body(row_count, column_count, adds, width, *refs):
    columns_end = row_count + column_count
    sums, outs = refs[columns_end : columns_end + row_count * adds], refs[-row_count:]
    rows = jnp.concatenate([ref[...] for ref in refs[:row_count]], axis=0)
    columns = jnp.concatenate([ref[...] for ref in refs[row_count:columns_end]], axis=0)
    probes = (rows.shape[1] - width) // 2
    row_scaled, column_scaled = rows[:, :width], columns[:, :width]
    row_norms = jnp.sum(row_scaled * row_scaled, axis=1, keepdims=True)
    ones = jnp.ones((8, width), jnp.float32)
    column_norms = dot(ones, column_scaled * column_scaled, ROWS_RULE)[:1]
    inner = dot(row_scaled, column_scaled, ROWS_RULE)
    kernel = jnp.exp(-0.5 * (row_norms + column_norms - 2.0 * inner))
    column_probes = columns[:, width : width + probes]
    swapped = jnp.concatenate([columns[:, width + probes :], column_probes], axis=1)
    weight = kernel * dot(rows[:, width:], swapped, ROWS_RULE)
    product = dot(kernel, column_probes)
    gradient = dot(weight, column_scaled) - jnp.sum(weight, axis=1, keepdims=True) * row_scaled
    points = outs[0].shape[0]
    for place, out in enumerate(outs):
        part = slice(place * points, (place + 1) * points)
        if adds:
            out[:, :width] = sums[place][:, :width] + gradient[part]
            out[:, width:] = sums[place][:, width:] + product[part]
        else:
            out[:, :width] = gradient[part]
            out[:, width:] = product[part]


def stage(rows, columns, sums, width):
    points, full = rows[0].shape
    probes = (full - width) // 2
    m, n = points * len(rows), points * len(columns)
    operands = [*rows, *columns, *(sums or ())]
    flops = 12 * m * n * (2 * width + 3 * probes)
    held = 4 * (6 * (m + n) * full + 8 * m * n)
    return pl.pallas_call(
        functools.partial(stage_body, len(rows), len(columns), bool(sums), width),
        out_shape=[jax.ShapeDtypeStruct((points, width + probes), jnp.float32)] * len(rows),
        in_specs=whole(len(operands)),
        out_specs=whole(len(rows)),
        compiler_params=pltpu.CompilerParams(vmem_limit_bytes=max(4 * MIB, held)),
        cost_estimate=pl.CostEstimate(
            flops=flops, bytes_accessed=4 * (m + n) * full, transcendentals=m * n
        ),
    )(*operands)


def total_body(*refs):
    parts, (product, gradient) = refs[:-2], refs[-2:]
    total = parts[0][...]
    for part in parts[1:]:
        total = total + part[...]
    gradient[...] = total[:, : gradient.shape[1]]
    product[...] = total[:, gradient.shape[1] :]


def total(parts, width):
    points, full = parts[0].shape
    return pl.pallas_call(
        total_body,
        out_shape=(
            jax.ShapeDtypeStruct((points, full - width), jnp.float32),
            jax.ShapeDtypeStruct((points, width), jnp.float32),
        ),
        in_specs=whole(len(parts)),
        out_specs=tuple(whole(2)),
        compiler_params=pltpu.CompilerParams(vmem_limit_bytes=4 * MIB),
    )(*parts)


def on_device(features, lengthscale, probes, cotangent):
    width = features.shape[1]
    places = lax.axis_size("blk") // CORES
    scaled = features / lengthscale[None, :]
    data = jnp.concatenate([scaled, probes, cotangent], axis=1)
    *early, late = gathered_line(data)
    rows = [data] + [over_plane(data, step) for step in range(places - 1, 0, -1)]
    sums = stage(rows, early + [over_cores(piece) for piece in early], None, width)
    sums = stage(rows, [late, over_cores(late)], sums, width)
    back = [over_plane(sums[places - step], step, True) for step in range(places - 1, 0, -1)]
    return total([sums[0]] + back, width)


def solution(mesh):
    spec = P(("blk", "sub"), None)
    return jax.shard_map(
        on_device, mesh=mesh, in_specs=(spec, P(), spec, spec), out_specs=(spec, spec), check_vma=False
    )
```

```python
import functools

import jax
import jax.numpy as jnp
from jax import lax
from jax.experimental import pallas as pl
from jax.experimental.pallas import tpu as pltpu
from jax.sharding import PartitionSpec as P

HIGH = lax.Precision.HIGHEST
ROWS_RULE = (((1,), (1,)), ((), ()))
PLAIN_RULE = (((1,), (0,)), ((), ()))
CORES = 2
LANES = 128
MIB = 2**20


def whole(count):
    return [pl.BlockSpec(memory_space=pltpu.VMEM)] * count


def dot(left, right, rule=PLAIN_RULE):
    return lax.dot_general(left, right, rule, precision=HIGH, preferred_element_type=jnp.float32)


def partner(position, step, length):
    if length & (length - 1) == 0:
        return position ^ step
    return (position + step) % length


def over_plane(value, step, back=False):
    blocks = lax.axis_size("blk")
    places = blocks // CORES
    pairs = [
        (p * CORES + c, partner(p, step, places) * CORES + c)
        for p in range(places)
        for c in range(CORES)
    ]
    return lax.ppermute(value, "blk", [(b, a) for a, b in pairs] if back else pairs)


def over_line(value, step):
    length = lax.axis_size("sub")
    return lax.ppermute(value, "sub", [(p, partner(p, step, length)) for p in range(length)])


def over_cores(value):
    return lax.ppermute(value, "blk", [(i, i ^ 1) for i in range(lax.axis_size("blk"))])


def gathered_line(value):
    length = lax.axis_size("sub")
    if length & (length - 1):
        return [value] + [over_line(value, step) for step in range(length - 1, 0, -1)]
    pieces, step = [value], length // 2
    while step:
        pieces = pieces + [over_line(piece, step) for piece in pieces]
        step //= 2
    return pieces


def stage_body(row_count, column_count, adds, width, *refs):
    columns_end = row_count + column_count
    sums, outs = refs[columns_end : columns_end + row_count * adds], refs[-row_count:]
    rows = jnp.concatenate([ref[...] for ref in refs[:row_count]], axis=0)
    columns = jnp.concatenate([ref[...] for ref in refs[row_count:columns_end]], axis=0)
    probes = (rows.shape[1] - width) // 2
    row_scaled, column_scaled = rows[:, :width], columns[:, :width]
    row_norms = jnp.sum(row_scaled * row_scaled, axis=1, keepdims=True)
    column_norms = jnp.sum(column_scaled * column_scaled, axis=1, keepdims=True)
    column_norms = jnp.broadcast_to(column_norms, (column_norms.shape[0], LANES)).T[:1]
    inner = dot(row_scaled, column_scaled, ROWS_RULE)
    kernel = jnp.exp(-0.5 * (row_norms + column_norms - 2.0 * inner))
    column_probes = columns[:, width : width + probes]
    swapped = jnp.concatenate([columns[:, width + probes :], column_probes], axis=1)
    weight = kernel * dot(rows[:, width:], swapped, ROWS_RULE)
    product = dot(kernel, column_probes)
    gradient = dot(weight, column_scaled) - jnp.sum(weight, axis=1, keepdims=True) * row_scaled
    points = outs[0].shape[0]
    for place, out in enumerate(outs):
        part = slice(place * points, (place + 1) * points)
        if adds:
            out[:, :width] = sums[place][:, :width] + gradient[part]
            out[:, width:] = sums[place][:, width:] + product[part]
        else:
            out[:, :width] = gradient[part]
            out[:, width:] = product[part]


def stage(rows, columns, sums, width):
    points, full = rows[0].shape
    probes = (full - width) // 2
    m, n = points * len(rows), points * len(columns)
    operands = [*rows, *columns, *(sums or ())]
    flops = 12 * m * n * (2 * width + 3 * probes)
    held = 4 * (6 * (m + n) * full + 8 * m * n)
    return pl.pallas_call(
        functools.partial(stage_body, len(rows), len(columns), bool(sums), width),
        out_shape=[jax.ShapeDtypeStruct((points, width + probes), jnp.float32)] * len(rows),
        in_specs=whole(len(operands)),
        out_specs=whole(len(rows)),
        compiler_params=pltpu.CompilerParams(vmem_limit_bytes=max(4 * MIB, held)),
        cost_estimate=pl.CostEstimate(
            flops=flops, bytes_accessed=4 * (m + n) * full, transcendentals=m * n
        ),
    )(*operands)


def total_body(*refs):
    parts, (product, gradient) = refs[:-2], refs[-2:]
    total = parts[0][...]
    for part in parts[1:]:
        total = total + part[...]
    gradient[...] = total[:, : gradient.shape[1]]
    product[...] = total[:, gradient.shape[1] :]


def total(parts, width):
    points, full = parts[0].shape
    return pl.pallas_call(
        total_body,
        out_shape=(
            jax.ShapeDtypeStruct((points, full - width), jnp.float32),
            jax.ShapeDtypeStruct((points, width), jnp.float32),
        ),
        in_specs=whole(len(parts)),
        out_specs=tuple(whole(2)),
        compiler_params=pltpu.CompilerParams(vmem_limit_bytes=4 * MIB),
    )(*parts)


def on_device(features, lengthscale, probes, cotangent):
    width = features.shape[1]
    places = lax.axis_size("blk") // CORES
    scaled = features / lengthscale[None, :]
    data = jnp.concatenate([scaled, probes, cotangent], axis=1)
    *early, late = gathered_line(data)
    rows = [data] + [over_plane(data, step) for step in range(places - 1, 0, -1)]
    sums = stage(rows, early + [over_cores(piece) for piece in early], None, width)
    sums = stage(rows, [late, over_cores(late)], sums, width)
    back = [over_plane(sums[places - step], step, True) for step in range(places - 1, 0, -1)]
    return total([sums[0]] + back, width)


def solution(mesh):
    spec = P(("blk", "sub"), None)
    return jax.shard_map(
        on_device, mesh=mesh, in_specs=(spec, P(), spec, spec), out_specs=(spec, spec), check_vma=False
    )
```

```python
import functools

import jax
import jax.numpy as jnp
from jax import lax
from jax.experimental import pallas as pl
from jax.experimental.pallas import tpu as pltpu
from jax.sharding import PartitionSpec as P

HIGH = lax.Precision.HIGHEST
ROWS_RULE = (((1,), (1,)), ((), ()))
PLAIN_RULE = (((1,), (0,)), ((), ()))
CORES = 2
LANES = 128
MIB = 2**20


def whole(count):
    return [pl.BlockSpec(memory_space=pltpu.VMEM)] * count


def dot(left, right, rule=PLAIN_RULE):
    return lax.dot_general(left, right, rule, precision=HIGH, preferred_element_type=jnp.float32)


def partner(position, step, length):
    if length & (length - 1) == 0:
        return position ^ step
    return (position + step) % length


def over_cores(value):
    return lax.ppermute(value, "blk", [(i, i ^ 1) for i in range(lax.axis_size("blk"))])


def to_chips(value, first, second, back=False):
    blocks, length = lax.axis_size("blk"), lax.axis_size("sub")
    pairs = []
    for b in range(blocks):
        place, core = b // CORES, b % CORES
        along_plane, along_line = (first, second)[core]
        there = partner(place, along_plane, blocks // CORES) * CORES + core
        pairs += [(b * length + s, there * length + partner(s, along_line, length)) for s in range(length)]
    return lax.ppermute(value, ("blk", "sub"), [(b, a) for a, b in pairs] if back else pairs)


def terms_body(count, mixed, mixed_columns, adds, width, core_ref, *refs):
    row_count, column_count = count
    rows = [ref[...] for ref in refs[:row_count]]
    columns = [ref[...] for ref in refs[row_count : row_count + column_count]]
    points = rows[0].shape[0]
    first = core_ref[0] == 0
    for place in range(1, row_count, 2):
        one, other = rows[place : place + 2]
        rows[place] = jnp.where(first, one, other)
        rows[place + 1] = jnp.where(first, other, one)
    if mixed:
        here, there = (ref[...] for ref in refs[row_count + column_count : row_count + column_count + 2])
        rows.append(jnp.where(first, here[:points], there[points:]))
        if mixed_columns:
            columns.append(jnp.where(first, there, here))
    operand_count = row_count + column_count + 2 * mixed
    sums = refs[operand_count : len(refs) - len(rows)]
    outs = refs[len(refs) - len(rows) :]
    rows, columns = jnp.concatenate(rows, axis=0), jnp.concatenate(columns, axis=0)
    probes = (rows.shape[1] - width) // 2
    row_scaled, column_scaled = rows[:, :width], columns[:, :width]
    row_norms = jnp.sum(row_scaled * row_scaled, axis=1, keepdims=True)
    column_norms = jnp.sum(column_scaled * column_scaled, axis=1, keepdims=True)
    column_norms = jnp.broadcast_to(column_norms, (column_norms.shape[0], LANES)).T[:1]
    inner = dot(row_scaled, column_scaled, ROWS_RULE)
    kernel = jnp.exp(-0.5 * (row_norms + column_norms - 2.0 * inner))
    column_probes = columns[:, width : width + probes]
    swapped = jnp.concatenate([columns[:, width + probes :], column_probes], axis=1)
    weight = kernel * dot(rows[:, width:], swapped, ROWS_RULE)
    product = dot(kernel, column_probes)
    gradient = dot(weight, column_scaled) - jnp.sum(weight, axis=1, keepdims=True) * row_scaled
    for place, out in enumerate(outs):
        part = slice(place * points, (place + 1) * points)
        if adds:
            out[:, :width] = sums[place][:, :width] + gradient[part]
            out[:, width:] = sums[place][:, width:] + product[part]
        else:
            out[:, :width] = gradient[part]
            out[:, width:] = product[part]


def terms(core, rows, columns, mixed, sums, width):
    points, full = rows[0].shape
    probes = (full - width) // 2
    row_count = len(rows) + bool(mixed)
    m, n = points * row_count, sum(p.shape[0] for p in columns) + (CORES * points if mixed and not sums else 0)
    operands = [*rows, *columns, *mixed, *(sums or ())]
    held = 4 * (8 * (m + n) * full + 8 * m * n)
    return pl.pallas_call(
        functools.partial(terms_body, (len(rows), len(columns)), bool(mixed), not sums, bool(sums), width),
        out_shape=[jax.ShapeDtypeStruct((points, width + probes), jnp.float32)] * row_count,
        in_specs=[pl.BlockSpec(memory_space=pltpu.SMEM)] + whole(len(operands)),
        out_specs=whole(row_count),
        compiler_params=pltpu.CompilerParams(vmem_limit_bytes=max(8 * MIB, held)),
        cost_estimate=pl.CostEstimate(
            flops=12 * m * n * (2 * width + 3 * probes), bytes_accessed=4 * (m + n) * full, transcendentals=m * n
        ),
    )(core, *operands)


def total_body(*refs):
    parts, (product, gradient) = refs[:-2], refs[-2:]
    total = parts[0][...]
    for part in parts[1:]:
        total = total + part[...]
    gradient[...] = total[:, : gradient.shape[1]]
    product[...] = total[:, gradient.shape[1] :]


def total(parts, width):
    points, full = parts[0].shape
    return pl.pallas_call(
        total_body,
        out_shape=(
            jax.ShapeDtypeStruct((points, full - width), jnp.float32),
            jax.ShapeDtypeStruct((points, width), jnp.float32),
        ),
        in_specs=whole(len(parts)),
        out_specs=tuple(whole(2)),
        compiler_params=pltpu.CompilerParams(vmem_limit_bytes=4 * MIB),
    )(*parts)


def in_twos(steps):
    return [(steps[i], steps[i + 1]) for i in range(0, len(steps) - 1, 2)]


def on_device(features, lengthscale, probes, cotangent):
    width, points = features.shape[1], features.shape[0]
    places, length = lax.axis_size("blk") // CORES, lax.axis_size("sub")
    core = (lax.axis_index("blk") % CORES).astype(jnp.int32).reshape(1)
    scaled = features / lengthscale[None, :]
    data = jnp.concatenate([scaled, probes, cotangent], axis=1)
    chip = jnp.concatenate([data, over_cores(data)], axis=0)
    line = [(0, step) for step in range(1, length)]
    plane = [(step, 0) for step in range(1, places)]
    rows, columns, mixed, ways, late = [data], [chip], [], [], []
    for first, second in in_twos(line):
        late.append(to_chips(chip, first, second))
    odd_line, odd_plane = line[len(line) // 2 * 2 :], plane[len(plane) // 2 * 2 :]
    if odd_line and odd_plane:
        got = to_chips(chip, odd_plane[0], odd_line[0])
        mixed = [got, over_cores(got)]
    elif odd_line:
        columns.append(to_chips(chip, odd_line[0], odd_line[0]))
    for first, second in in_twos(plane):
        got = to_chips(chip, second, first)
        rows += [got[:points], over_cores(got[points:])]
        ways += [(second, second), (first, first)]
    if odd_plane:
        ways.append((odd_plane[0], odd_plane[0]))
        if not mixed:
            rows.append(to_chips(data, odd_plane[0], odd_plane[0]))
    sums = terms(core, rows, columns, mixed, None, width)
    late, sums = lax.optimization_barrier((late, sums))
    if late:
        late += [over_cores(piece) for piece in late]
        sums = terms(core, rows, late, mixed, sums, width)
    own, *others = sums
    returns = list(zip(others, ways))
    back = [to_chips(part, *way, back=True) for part, way in returns[-1:] + returns[:-1]]
    return total([own] + back, width)


def solution(mesh):
    spec = P(("blk", "sub"), None)
    return jax.shard_map(
        on_device, mesh=mesh, in_specs=(spec, P(), spec, spec), out_specs=(spec, spec), check_vma=False
    )
```

```python
import functools

import jax
import jax.numpy as jnp
from jax import lax
from jax.experimental import pallas as pl
from jax.experimental.pallas import tpu as pltpu
from jax.sharding import PartitionSpec as P

HIGH = lax.Precision.HIGHEST
ROWS_RULE = (((1,), (1,)), ((), ()))
PLAIN_RULE = (((1,), (0,)), ((), ()))
CORES = 2
LANES = 128
MIB = 2**20


def whole(count):
    return [pl.BlockSpec(memory_space=pltpu.VMEM)] * count


def dot(left, right, rule=PLAIN_RULE):
    return lax.dot_general(left, right, rule, precision=HIGH, preferred_element_type=jnp.float32)


def partner(position, step, length):
    if length & (length - 1) == 0:
        return position ^ step
    return (position + step) % length


def over_cores(value):
    return lax.ppermute(value, "blk", [(i, i ^ 1) for i in range(lax.axis_size("blk"))])


def to_chips(value, first, second, back=False):
    blocks, length = lax.axis_size("blk"), lax.axis_size("sub")
    pairs = []
    for b in range(blocks):
        place, core = b // CORES, b % CORES
        along_plane, along_line = (first, second)[core]
        there = partner(place, along_plane, blocks // CORES) * CORES + core
        pairs += [(b * length + s, there * length + partner(s, along_line, length)) for s in range(length)]
    return lax.ppermute(value, ("blk", "sub"), [(b, a) for a, b in pairs] if back else pairs)


def terms_body(count, mixed, mixed_columns, adds, width, core_ref, *refs):
    row_count, column_count = count
    rows = [ref[...] for ref in refs[:row_count]]
    columns = [ref[...] for ref in refs[row_count : row_count + column_count]]
    points = rows[0].shape[0]
    first = core_ref[0] == 0
    for place in range(1, row_count, 2):
        one, other = rows[place : place + 2]
        rows[place] = jnp.where(first, one, other)
        rows[place + 1] = jnp.where(first, other, one)
    if mixed:
        here, there = (ref[...] for ref in refs[row_count + column_count : row_count + column_count + 2])
        rows.append(jnp.where(first, here[:points], there[points:]))
        if mixed_columns:
            columns.append(jnp.where(first, there, here))
    operand_count = row_count + column_count + 2 * mixed
    sums = refs[operand_count : len(refs) - len(rows)]
    outs = refs[len(refs) - len(rows) :]
    rows, columns = jnp.concatenate(rows, axis=0), jnp.concatenate(columns, axis=0)
    probes = (rows.shape[1] - width) // 2
    row_scaled, column_scaled = rows[:, :width], columns[:, :width]
    row_norms = jnp.sum(row_scaled * row_scaled, axis=1, keepdims=True)
    column_norms = jnp.sum(column_scaled * column_scaled, axis=1, keepdims=True)
    column_norms = jnp.broadcast_to(column_norms, (column_norms.shape[0], LANES)).T[:1]
    inner = dot(row_scaled, column_scaled, ROWS_RULE)
    kernel = jnp.exp(-0.5 * (row_norms + column_norms - 2.0 * inner))
    column_probes = columns[:, width : width + probes]
    swapped = jnp.concatenate([columns[:, width + probes :], column_probes], axis=1)
    weight = kernel * dot(rows[:, width:], swapped, ROWS_RULE)
    product = dot(kernel, column_probes)
    gradient = dot(weight, column_scaled) - jnp.sum(weight, axis=1, keepdims=True) * row_scaled
    for place, out in enumerate(outs):
        part = slice(place * points, (place + 1) * points)
        if adds:
            out[:, :width] = sums[place][:, :width] + gradient[part]
            out[:, width:] = sums[place][:, width:] + product[part]
        else:
            out[:, :width] = gradient[part]
            out[:, width:] = product[part]


def terms(core, rows, columns, mixed, sums, width):
    points, full = rows[0].shape
    probes = (full - width) // 2
    row_count = len(rows) + bool(mixed)
    m, n = points * row_count, sum(p.shape[0] for p in columns) + (CORES * points if mixed and not sums else 0)
    operands = [*rows, *columns, *mixed, *(sums or ())]
    held = 4 * (8 * (m + n) * full + 8 * m * n)
    return pl.pallas_call(
        functools.partial(terms_body, (len(rows), len(columns)), bool(mixed), not sums, bool(sums), width),
        out_shape=[jax.ShapeDtypeStruct((points, width + probes), jnp.float32)] * row_count,
        in_specs=[pl.BlockSpec(memory_space=pltpu.SMEM)] + whole(len(operands)),
        out_specs=whole(row_count),
        compiler_params=pltpu.CompilerParams(vmem_limit_bytes=max(8 * MIB, held)),
        cost_estimate=pl.CostEstimate(
            flops=12 * m * n * (2 * width + 3 * probes), bytes_accessed=4 * (m + n) * full, transcendentals=m * n
        ),
    )(core, *operands)


def total_body(*refs):
    parts, (product, gradient) = refs[:-2], refs[-2:]
    total = parts[0][...]
    for part in parts[1:]:
        total = total + part[...]
    gradient[...] = total[:, : gradient.shape[1]]
    product[...] = total[:, gradient.shape[1] :]


def total(parts, width):
    points, full = parts[0].shape
    return pl.pallas_call(
        total_body,
        out_shape=(
            jax.ShapeDtypeStruct((points, full - width), jnp.float32),
            jax.ShapeDtypeStruct((points, width), jnp.float32),
        ),
        in_specs=whole(len(parts)),
        out_specs=tuple(whole(2)),
        compiler_params=pltpu.CompilerParams(vmem_limit_bytes=4 * MIB),
    )(*parts)


def in_twos(steps):
    return [(steps[i], steps[i + 1]) for i in range(0, len(steps) - 1, 2)]


def on_device(features, lengthscale, probes, cotangent):
    width, points = features.shape[1], features.shape[0]
    places, length = lax.axis_size("blk") // CORES, lax.axis_size("sub")
    core = (lax.axis_index("blk") % CORES).astype(jnp.int32).reshape(1)
    scaled = features / lengthscale[None, :]
    data = jnp.concatenate([scaled, probes, cotangent], axis=1)
    chip = jnp.concatenate([data, over_cores(data)], axis=0)
    line = [(0, step) for step in range(1, length)]
    plane = [(step, 0) for step in range(1, places)]
    rows, columns, mixed, ways, late = [data], [chip], [], [], []
    for first, second in in_twos(line):
        late.append(to_chips(chip, first, second))
    odd_line, odd_plane = line[len(line) // 2 * 2 :], plane[len(plane) // 2 * 2 :]
    if odd_line and odd_plane:
        got = to_chips(chip, odd_plane[0], odd_line[0])
        mixed = [got, over_cores(got)]
    elif odd_line:
        columns.append(to_chips(chip, odd_line[0], odd_line[0]))
    for first, second in in_twos(plane):
        got = to_chips(chip, second, first)
        rows += [got[:points], over_cores(got[points:])]
        ways += [(second, second), (first, first)]
    if odd_plane:
        ways.append((odd_plane[0], odd_plane[0]))
        if not mixed:
            rows.append(to_chips(data, odd_plane[0], odd_plane[0]))
    sums = terms(core, rows, columns, mixed, None, width)
    late, sums = lax.optimization_barrier((late, sums))
    if late:
        swapped = [over_cores(piece) for piece in late]
        sums = terms(core, rows, late, mixed, sums, width)
        sums = terms(core, rows, swapped, mixed, sums, width)
    own, *others = sums
    returns = list(zip(others, ways))
    back = [to_chips(part, *way, back=True) for part, way in returns[-1:] + returns[:-1]]
    return total([own] + back, width)


def solution(mesh):
    spec = P(("blk", "sub"), None)
    return jax.shard_map(
        on_device, mesh=mesh, in_specs=(spec, P(), spec, spec), out_specs=(spec, spec), check_vma=False
    )
```
